512 devices in a mesh: space: 128 (over z, x, core), col: 4 (over y).
Axes of the slice: x: 4, y: 4, z: 16, core: 2. Of those that a mesh axis runs over, the one named last changes fastest.
Arguments:
- edge_embed: bfloat16 [16384, 512], P('space', 'col'), may hold values from -6 to 6
- atom_embed: bfloat16 [1024, 256], P('space'), may hold values from -6 to 6
- cotangent: bfloat16 [16384, 512], P('space', 'col'), may hold values from -6 to 6
- trip_basis: bfloat16 [524288, 64], P('space'), may hold values from -6 to 6
- weight_in: bfloat16 [512, 512], P(None, 'col'), may hold values from -0.21875 to 0.21875
- weight_atom: bfloat16 [256, 512], P(None, 'col'), may hold values from -0.21875 to 0.21875
- weight_basis: bfloat16 [64, 512], P(None, 'col'), may hold values from -0.125 to 0.125
- weight_out: bfloat16 [512, 512], P(None, 'col'), may hold values from -0.25 to 0.25
- atom_index: int32 [16384], P('space'), may hold values from 0 to 7
- trip_source: int32 [524288], P('space'), may hold values from 0 to 1151, as said below
- trip_target: int32 [524288], P('space'), may hold values from 0 to 127
- send_rows: int32 [128, 1024], P('space'), may hold values from 0 to 127
Outputs:
- grad_edge: bfloat16 [16384, 512], P('space', 'col')
- grad_atom: float32 [1024, 256], P('space')
- grad_w_in: float32 [512, 512], P(None, 'col')
- grad_w_atom: float32 [256, 512], P(None, 'col')
- grad_w_basis: float32 [64, 512], P(None, 'col')
- grad_w_out: float32 [512, 512], P(None, 'col')
The draws below stay inside these ranges and needn't reach their ends.
Inputs may be any that keep to these rules, and one draw needn't show every extreme that they name: `trip_source`: index into the region's 128 edges followed by its 1024 boundary slots (slot j from region s at 128 + s * 8 + j). For each pair of regions only the first 1 to 8 slots are ever referenced; that count is 8 from both neighbouring regions (s = r - 1 and r + 1, modulo 128) and 0 from the region itself.
All inputs are finite; a program needn't handle non-finite values.
Results may differ from the reference program's by a relative error of at most 0.006.
Values may be sent and summed in bfloat16 or wider, within the bound.
No kernel may reach another device: no remote copies, remote signals or barrier semaphores. Data moves between devices by JAX's collectives and lax.ppermute only.
A program may use at most 64 MiB of HBM per device.

```python
import math
import jax
import jax.numpy as jnp
from jax import lax

D = 512
AW = 256
NB = 64
EDGE_DEV = 128
TRIP_BLK = 4096
CAP = 8
ATOM_DEV = 8
HALO = 1024
EDGES = 16384
ATOMS = 1024
TRIPLETS = 524288
N_SPACE = 128


def draw_trip_source(key, part):
    key = jax.random.fold_in(key, 7)
    count_key, flat_key, pick_key, local_key = jax.random.split(key, 4)
    device_count = N_SPACE
    halo = device_count * CAP
    trips = EDGE_DEV // 128 * TRIP_BLK
    dev_ids = jnp.arange(device_count, dtype=jnp.int32)
    counts = jax.random.randint(count_key, (device_count, device_count), 1, CAP + 1)
    below = dev_ids[:, None] == (dev_ids[None, :] + 1) % device_count
    above = dev_ids[:, None] == (dev_ids[None, :] - 1) % device_count
    counts = jnp.where(below | above, CAP, counts)
    counts = jnp.where(dev_ids[:, None] == dev_ids[None, :], 0, counts)
    flat_slot = jax.random.randint(flat_key, (device_count, trips), 0, halo)
    sender_id = flat_slot // CAP
    slot_index = flat_slot % CAP
    allowed = slot_index < counts[sender_id, dev_ids[:, None]]
    picked = jax.random.randint(pick_key, (device_count, trips), 0, 2) == 0
    local_rows = jax.random.randint(local_key, (device_count, trips), 0, EDGE_DEV)
    chosen = jnp.where(picked & allowed, EDGE_DEV + flat_slot, local_rows)
    chosen = chosen.at[:, 0].set(EDGE_DEV + (dev_ids - 1) % device_count * CAP + CAP - 1)
    chosen = chosen.at[:, 1].set(0)
    return chosen.reshape(device_count * trips).astype(jnp.int32)


def set_ends(entries, own_key, low, high):
    extent = entries.shape
    place = [jax.random.randint(jax.random.fold_in(own_key, axis), (), 0, extent[axis]) for axis in range(len(extent))]
    entries = entries.at[tuple(place)].set(low)
    longest = extent.index(max(extent))
    place[longest] = (place[longest] + 1) % extent[longest]
    return entries.at[tuple(place)].set(high)


def shard_levels(key, dims, cuts, smallest, largest):
    loudness = 1.0
    for position, parts in cuts:
        heights = jax.random.uniform(jax.random.fold_in(jax.random.fold_in(key, 6), position), (parts,), jnp.float32, smallest / len(cuts), largest / len(cuts))
        loudness = loudness * jnp.repeat(jnp.exp(heights), dims[position] // parts).reshape((-1,) + (1,) * (len(dims) - 1 - position))
    return loudness


def scatter_about(own_key, extent, scale, bound, cuts=(), kind=jnp.bfloat16):
    values = jax.random.normal(own_key, extent, jnp.float32) * scale
    if len(cuts) > 0:
        values = shard_levels(own_key, extent, cuts, -0.22, 0.18) * values
    return jnp.clip(values, min=-bound, max=bound).astype(kind)


def setup_inputs(seed: int = 0) -> dict:
    arg_keys = jax.random.split(jax.random.key(seed), 13)
    edge_embed = scatter_about(arg_keys[0], (EDGES, D), 1.0, 6.0, ((0, 128), (1, 4)))
    atom_embed = scatter_about(arg_keys[1], (ATOMS, AW), 1.0, 6.0, ((0, 128),))
    cotangent = scatter_about(arg_keys[2], (EDGES, D), 1.0, 6.0, ((0, 128), (1, 4)))
    trip_basis = scatter_about(arg_keys[3], (TRIPLETS, NB), 1.0, 6.0, ((0, 128),))
    weight_in = scatter_about(arg_keys[4], (D, D), (D + AW) ** -0.5, 0.21875, ((1, 4),))
    weight_atom = scatter_about(arg_keys[5], (AW, D), (D + AW) ** -0.5, 0.21875, ((1, 4),))
    weight_basis = scatter_about(arg_keys[6], (NB, D), (NB * TRIP_BLK // 128) ** -0.5, 0.125, ((1, 4),))
    weight_out = scatter_about(arg_keys[7], (D, D), D ** -0.5, 0.25, ((1, 4),))
    atom_index = set_ends(jax.random.randint(arg_keys[8], (EDGES,), 0, ATOM_DEV), jax.random.fold_in(arg_keys[8], 1), 0, ATOM_DEV - 1).astype(jnp.int32)
    trip_source = draw_trip_source(jax.random.fold_in(arg_keys[12], 71), 0)
    trip_target = set_ends(jax.random.randint(arg_keys[10], (TRIPLETS,), 0, 128), jax.random.fold_in(arg_keys[10], 1), 0, 127).astype(jnp.int32)
    send_rows = set_ends(jax.random.randint(arg_keys[11], (N_SPACE, HALO), 0, EDGE_DEV), jax.random.fold_in(arg_keys[11], 1), 0, EDGE_DEV - 1).astype(jnp.int32)
    return dict(edge_embed=edge_embed, atom_embed=atom_embed, cotangent=cotangent, trip_basis=trip_basis, weight_in=weight_in, weight_atom=weight_atom, weight_basis=weight_basis, weight_out=weight_out, atom_index=atom_index, trip_source=trip_source, trip_target=trip_target, send_rows=send_rows)


def silu_slope(preact):
    sigmoid_pre = jax.nn.sigmoid(preact)
    return sigmoid_pre * (1.0 + preact * (1.0 - sigmoid_pre))

def reference(edge_embed, atom_embed, cotangent, trip_basis, weight_in, weight_atom, weight_basis, weight_out, atom_index, trip_source, trip_target, send_rows):
    device_count = N_SPACE
    trips = EDGE_DEV // 128 * TRIP_BLK
    halo = device_count * CAP
    grad_scale = 1.0 / math.sqrt(EDGES)
    dev_ids = jnp.arange(device_count, dtype=jnp.int32)
    atom_local = atom_index.reshape(device_count, EDGE_DEV)
    atom_global = (atom_local + dev_ids[:, None] * ATOM_DEV).reshape(EDGES).astype(jnp.int32)
    atom_edge = atom_embed[atom_global]
    preact = jnp.dot(edge_embed, weight_in, preferred_element_type=jnp.float32) + jnp.dot(atom_edge, weight_atom, preferred_element_type=jnp.float32)
    active = jax.nn.silu(preact).astype(jnp.bfloat16).reshape(device_count, EDGE_DEV, D)
    grad_msg = jnp.dot(cotangent, weight_out.T, preferred_element_type=jnp.float32).astype(jnp.bfloat16).reshape(device_count, EDGE_DEV, D)
    sources = trip_source.reshape(device_count, trips)
    offsets = (jnp.arange(trips, dtype=jnp.int32) // TRIP_BLK * 128).astype(jnp.int32)
    targets = (trip_target.reshape(device_count, trips) + offsets[None, :]).astype(jnp.int32)
    basis_in = trip_basis.reshape(device_count, trips, NB)

    def per_device(running, device):
        grad_act, grad_bw = running
        rows_in = lax.dynamic_slice_in_dim(send_rows, (device * CAP).astype(jnp.int32), CAP, 1)
        incoming = active[dev_ids[:, None], rows_in].reshape(halo, D)
        extended = jnp.concatenate([active[device], incoming], axis=0)
        source = sources[device]
        target = targets[device]
        basis_here = basis_in[device]
        basis_val = jnp.dot(basis_here, weight_basis, preferred_element_type=jnp.float32)
        gathered = extended[source].astype(jnp.float32)
        product = (basis_val * gathered).astype(jnp.bfloat16)
        message = jax.ops.segment_sum(product.astype(jnp.float32), target, num_segments=EDGE_DEV).astype(jnp.bfloat16)
        spread = grad_msg[device][target].astype(jnp.float32)
        grad_basis = (spread * gathered).astype(jnp.bfloat16)
        grad_bw = grad_bw + jnp.dot(basis_here.T, grad_basis, preferred_element_type=jnp.float32)
        grad_ext = jax.ops.segment_sum(spread * basis_val, source, num_segments=EDGE_DEV + halo)
        grad_act = grad_act.at[device].add(grad_ext[:EDGE_DEV])
        grad_act = grad_act.at[dev_ids[:, None], rows_in].add(grad_ext[EDGE_DEV:].reshape(device_count, CAP, D))
        return ((grad_act, grad_bw), message)
    start = (jnp.zeros((device_count, EDGE_DEV, D), jnp.float32), jnp.zeros((NB, D), jnp.float32))
    (grad_act, grad_bw), messages = lax.scan(per_device, start, dev_ids)
    grad_pre = (grad_act.reshape(EDGES, D) * silu_slope(preact)).astype(jnp.bfloat16)
    grad_edge = jnp.dot(grad_pre, weight_in.T, preferred_element_type=jnp.float32).astype(jnp.bfloat16)
    partial_atom = jnp.dot(grad_pre, weight_atom.T, preferred_element_type=jnp.float32)
    grad_atom = jax.ops.segment_sum(partial_atom, atom_global, num_segments=ATOMS)
    messages = messages.reshape(EDGES, D)
    grad_w_in = jnp.dot(edge_embed.T, grad_pre, preferred_element_type=jnp.float32) * grad_scale
    grad_w_atom = jnp.dot(atom_edge.T, grad_pre, preferred_element_type=jnp.float32) * grad_scale
    grad_w_out = jnp.dot(messages.T, cotangent, preferred_element_type=jnp.float32) * grad_scale
    grad_w_basis = grad_bw * grad_scale
    return (grad_edge, grad_atom, grad_w_in, grad_w_atom, grad_w_basis, grad_w_out)
```

```python
import functools
import math

import jax
import jax.numpy as jnp
from jax import lax
from jax.experimental import pallas as pl
from jax.experimental.pallas import tpu as pltpu
from jax.sharding import PartitionSpec as P

F32 = jnp.float32
BF16 = jnp.bfloat16
VMEM = pl.BlockSpec(memory_space=pltpu.VMEM)
ROWS = 1408
STEP = 512


def call(kernel, outs, *args, scratch=(), flops=0):
    total = sum(math.prod(o.shape) * o.dtype.itemsize for o in outs)
    total += sum(a.size * a.dtype.itemsize for a in args)
    return pl.pallas_call(
        kernel,
        out_shape=list(outs),
        in_specs=[VMEM] * len(args),
        out_specs=[VMEM] * len(outs),
        scratch_shapes=list(scratch),
        compiler_params=pltpu.CompilerParams(vmem_limit_bytes=40 * 1024 * 1024),
        cost_estimate=pl.CostEstimate(flops=flops, bytes_accessed=total, transcendentals=0),
    )(*args)


def shape(*dims, dtype=F32):
    return jax.ShapeDtypeStruct(dims, dtype)


def dot(a, b, dims=((1,), (0,))):
    return lax.dot_general(a, b, (dims, ((), ())), preferred_element_type=F32)


def dot_nt(a, b):
    return dot(a, b, ((1,), (1,)))


def dot_tn(a, b):
    return dot(a, b, ((0,), (0,)))


def one_hot(mask):
    return jnp.where(mask, 1.0, 0.0).astype(BF16)


def iota(rows, lanes, axis):
    return lax.broadcasted_iota(jnp.int32, (rows, lanes), axis)


def block_of(ref, index):
    return ref[pl.ds(pl.multiple_of(index * 128, 128), 128), :]


def near(distance):
    return lax.axis_index("col") ^ distance


def bit_of(level):
    return lax.rem(lax.axis_index("space") // (1 << level), 2)


def sigmoid(value):
    return 1.0 / (1.0 + jnp.exp(-value))


def edge_kernel(
    edge_ref, atom_ref, win_ref, watom_ref, index_ref, send_ref,
    pre_ref, act_ref, out_ref, ae_ref,
):
    index = index_ref[...]
    at = one_hot(iota(8, 128, 0) == index)
    atom_edge = dot_tn(at, atom_ref[...]).astype(BF16)
    ae_ref[...] = atom_edge
    pre = dot(atom_edge, watom_ref[...])
    for c in range(4):
        pre = pre + dot(edge_ref[c], win_ref[c * 128 : (c + 1) * 128, :])
    pre_ref[...] = pre
    act = (pre * sigmoid(pre)).astype(BF16)
    act_ref[...] = act
    for i in range(8):
        pick = one_hot(iota(128, 128, 0) == send_ref[i : i + 1, :])
        out_ref[i * 128 : (i + 1) * 128, :] = dot_tn(pick, act).astype(BF16)


def scatter_kernel(
    cot_ref, wout_ref, basis_ref, wb_ref, source_ref, target_ref,
    gm_ref, own_ref, halo_ref, acc_ref,
):
    mine = pl.ds(pl.multiple_of(lax.axis_index("col") * 128, 128), 128)
    total = dot_nt(cot_ref[0], wout_ref[0, mine, :])
    for c in range(1, 4):
        total = total + dot_nt(cot_ref[c], wout_ref[c, mine, :])
    gm = total.astype(BF16)
    gm_ref[...] = gm
    wb = wb_ref[...]
    rows = acc_ref.shape[0]
    for c in range(source_ref.shape[0] * 128 // STEP):
        lines = range(c * STEP // 128, (c + 1) * STEP // 128)
        basis = basis_ref[:, c * STEP : (c + 1) * STEP]
        bv = dot_tn(basis, wb)
        sel = jnp.concatenate(
            [one_hot(iota(128, 128, 0) == target_ref[i : i + 1, :]) for i in lines], axis=1
        )
        spread = dot_tn(sel, gm)
        exact = spread * bv
        high = exact.astype(BF16)
        low = (exact - high.astype(F32)).astype(BF16)
        put = jnp.concatenate(
            [one_hot(iota(rows, 128, 0) == source_ref[i : i + 1, :]) for i in lines], axis=1
        )
        both = dot(put, jnp.concatenate([high, low], axis=1))
        part = both[:, :128] + both[:, 128:]
        if c == 0:
            acc_ref[...] = part
        else:
            acc_ref[...] += part
    own_ref[...] = acc_ref[:128, :]
    halo_ref[...] = acc_ref[128:, :].astype(BF16)


def gather_kernel(
    act_ref, in_ref, gm_ref, basis_ref, wb_ref, source_ref, target_ref,
    msg_ref, bw_ref, ext_ref,
):
    ext_ref[:128, :] = act_ref[...]
    ext_ref[128:, :] = in_ref[...]
    ext = ext_ref[...]
    gm = gm_ref[...]
    wb = wb_ref[...]
    rows = ext_ref.shape[0]
    msg = jnp.zeros((128, 128), F32)
    bw = jnp.zeros(bw_ref.shape, F32)
    for c in range(source_ref.shape[0] * 128 // STEP):
        lines = range(c * STEP // 128, (c + 1) * STEP // 128)
        basis = basis_ref[:, c * STEP : (c + 1) * STEP]
        bv = dot_tn(basis, wb)
        sel = jnp.concatenate(
            [one_hot(iota(128, 128, 0) == target_ref[i : i + 1, :]) for i in lines], axis=1
        )
        spread = dot_tn(sel, gm)
        cols = jnp.concatenate(
            [jnp.broadcast_to(source_ref[i : i + 1, :], (128, 128)).T for i in lines], axis=0
        )
        pick = jnp.concatenate(
            [one_hot(cols == iota(STEP, 128, 1) + 128 * k) for k in range(rows // 128)], axis=1
        )
        z = dot(pick, ext)
        msg = msg + dot(sel, (bv * z).astype(BF16))
        bw = bw + dot(basis, (spread * z).astype(BF16))
    msg_ref[...] = msg.astype(BF16)
    bw_ref[...] = bw


def weight_kernel(
    ret_ref, own_ref, pre_ref, send_ref, edge_ref, ae_ref, win_ref, watom_ref, index_ref,
    msg_ref, cot_ref, bw_ref,
    out_ref, keep_ref, col_send, col_keep, acc_ref,
):
    ga = own_ref[...]
    for i in range(8):
        put = one_hot(iota(128, 128, 0) == send_ref[i : i + 1, :])
        ga = ga + dot(put, ret_ref[i * 128 : (i + 1) * 128, :])
    pre = pre_ref[...]
    sig = sigmoid(pre)
    gp = (ga * (sig * (1.0 + pre * (1.0 - sig)))).astype(BF16)
    cot = cot_ref[...]
    for c in range(4):
        acc_ref[c * 128 : (c + 1) * 128, :] = dot_tn(edge_ref[c], gp)
        acc_ref[768 + c * 128 : 896 + c * 128, :] = dot_tn(msg_ref[c], cot)
    acc_ref[512:768, :] = dot_tn(ae_ref[...], gp)
    acc_ref[1280:1344, :] = bw_ref[...]
    acc_ref[1344:, :] = jnp.zeros((ROWS - 1344, 128), F32)
    half = ROWS // 2
    mine = pl.multiple_of(bit_of(0) * half, 16)
    other = pl.multiple_of(half - mine, 16)
    keep_ref[...] = acc_ref[pl.ds(mine, half), :]
    out_ref[...] = acc_ref[pl.ds(other, half), :].astype(BF16)
    at = one_hot(iota(8, 128, 0) == index_ref[...])
    total = dot(at, gp)
    high = total.astype(BF16)
    low = (total - high.astype(F32)).astype(BF16)
    atom = dot_nt(high, watom_ref[...]) + dot_nt(low, watom_ref[...])
    col_keep[:128, :] = dot_nt(gp, block_of(win_ref, near(0)))
    col_keep[128:256, :] = dot_nt(gp, block_of(win_ref, near(2)))
    col_send[:128, :] = dot_nt(gp, block_of(win_ref, near(1))).astype(BF16)
    col_send[128:256, :] = dot_nt(gp, block_of(win_ref, near(3))).astype(BF16)
    split_atom(jnp.concatenate([atom[:, :128], atom[:, 128:]], axis=0), col_keep, col_send, 256)


def split_atom(atom, keep_ref, send_ref, place):
    high = atom.astype(BF16)
    low = (atom - high.astype(F32)).astype(BF16)
    send_ref[place : place + 16, :] = high
    send_ref[place + 16 : place + 32, :] = low
    keep_ref[place : place + 16, :] = high.astype(F32) + low.astype(F32)


def atom_sum(keep_ref, got_ref, place):
    high = got_ref[place : place + 16, :].astype(F32)
    return keep_ref[place : place + 16, :] + (high + got_ref[place + 16 : place + 32, :].astype(F32))


def col_kernel(keep_ref, got_ref, send_ref, own_ref):
    own_ref[:128, :] = keep_ref[:128, :] + got_ref[:128, :].astype(F32)
    send_ref[:128, :] = (keep_ref[128:256, :] + got_ref[128:256, :].astype(F32)).astype(BF16)
    split_atom(atom_sum(keep_ref, got_ref, 256), own_ref, send_ref, 128)


def col_final_kernel(keep_ref, got_ref, edge_ref, atom_ref):
    edge_ref[...] = (keep_ref[:128, :] + got_ref[:128, :].astype(F32)).astype(BF16)
    atom = atom_sum(keep_ref, got_ref, 128)
    atom_ref[:, :128] = atom[:8, :]
    atom_ref[:, 128:] = atom[8:, :]


def halve_kernel(level, keep_ref, got_ref, after_ref, send_ref, own_ref):
    half = send_ref.shape[0]
    mine = pl.multiple_of(bit_of(level) * half, 16)
    other = pl.multiple_of(half - mine, 16)
    send_ref[...] = (
        keep_ref[pl.ds(other, half), :] + got_ref[pl.ds(other, half), :].astype(F32)
    ).astype(BF16)
    own_ref[...] = keep_ref[pl.ds(mine, half), :] + got_ref[pl.ds(mine, half), :].astype(F32)


def add_kernel(own_ref, got_ref, after_ref, out_ref):
    out_ref[...] = (own_ref[...] + got_ref[...].astype(F32)).astype(BF16)


def z_sum_kernel(all_ref, out_ref):
    total = all_ref[0].astype(F32)
    for i in range(1, all_ref.shape[0]):
        total = total + all_ref[i].astype(F32)
    out_ref[...] = total.astype(BF16)


def final_kernel(scale, all_ref, win_ref, watom_ref, wb_ref, wout_ref, acc_ref):
    rows = all_ref.shape[1]
    for g in range(8):
        place = ((g % 2) * 4 + (g // 2 % 2) * 2 + g // 4) * rows
        acc_ref[place : place + rows, :] = all_ref[g].astype(F32) * scale
    win_ref[...] = acc_ref[:512, :]
    watom_ref[...] = acc_ref[512:768, :]
    wout_ref[...] = acc_ref[768:1280, :]
    wb_ref[...] = acc_ref[1280:1344, :]


def col_swap(array, distance):
    return lax.ppermute(array, "col", [(i, i ^ distance) for i in range(4)])


def space_swap(array, distance, extent):
    return lax.ppermute(array, "space", [(i, i ^ distance) for i in range(extent)])


def body(
    edge_embed,
    atom_embed,
    cotangent,
    trip_basis,
    weight_in,
    weight_atom,
    weight_basis,
    weight_out,
    atom_index,
    trip_source,
    trip_target,
    send_rows,
):
    extent = lax.axis_size("space")
    grad_scale = 1.0 / math.sqrt(edge_embed.shape[0] * extent)
    half = dict(dtype=BF16)
    source = trip_source.reshape(-1, 128)
    target = trip_target.reshape(-1, 128)
    send = send_rows.reshape(8, 128)
    index = atom_index.reshape(1, 128)

    basis = trip_basis.T
    edge_all = lax.all_gather(edge_embed, "col")
    cot_all = lax.all_gather(cotangent, "col")
    wout_all = lax.all_gather(weight_out, "col")
    preact, active, outgoing, atom_edge = call(
        edge_kernel,
        [shape(128, 128), shape(128, 128, **half), shape(1024, 128, **half), shape(128, 256, **half)],
        edge_all, atom_embed, weight_in, weight_atom, index, send,
    )
    incoming = lax.all_to_all(
        outgoing.reshape(extent, 8, 128), "space", split_axis=0, concat_axis=0, tiled=True
    ).reshape(1024, 128)
    grad_msg, grad_own, grad_halo = call(
        scatter_kernel,
        [shape(128, 128, **half), shape(128, 128), shape(1024, 128, **half)],
        cot_all, wout_all, basis, weight_basis, source, target,
        scratch=[pltpu.VMEM((1152, 128), F32)],
        flops=2 * 4096 * 1152 * 128,
    )
    returned = lax.all_to_all(
        grad_halo.reshape(extent, 8, 128), "space", split_axis=0, concat_axis=0, tiled=True
    ).reshape(1024, 128)
    message, grad_bw = call(
        gather_kernel,
        [shape(128, 128, **half), shape(64, 128)],
        active, incoming, grad_msg, basis, weight_basis, source, target,
        scratch=[pltpu.VMEM((1152, 128), BF16)],
        flops=2 * 4096 * 1152 * 128,
    )
    msg_all = lax.all_gather(message, "col")
    out, keep, col_out, col_keep = call(
        weight_kernel,
        [
            shape(ROWS // 2, 128, **half), shape(ROWS // 2, 128),
            shape(288, 128, **half), shape(272, 128),
        ],
        returned, grad_own, preact, send, edge_all, atom_edge, weight_in, weight_atom, index,
        msg_all, cotangent, grad_bw,
        scratch=[pltpu.VMEM((ROWS, 128), F32)],
    )
    rows = ROWS // 2
    after = col_keep
    for level in (1, 2):
        rows //= 2
        got = space_swap(out, 1 << (level - 1), extent)
        out, keep = call(
            functools.partial(halve_kernel, level),
            [shape(rows, 128, **half), shape(rows, 128)],
            keep, got, after,
        )
        if level == 1:
            col_out, col_keep = call(
                col_kernel, [shape(160, 128, **half), shape(144, 128)], col_keep, col_swap(col_out, 1)
            )
            after = col_keep
    grad_edge, grad_atom = call(
        col_final_kernel, [shape(128, 128, **half), shape(8, 256)], col_keep, col_swap(col_out, 2)
    )
    (out,) = call(
        add_kernel, [shape(rows, 128, **half)], keep, space_swap(out, 4, extent), grad_atom
    )
    groups = [[z * 8 + g for z in range(extent // 8)] for g in range(8)]
    out = lax.all_gather(out, "space", axis_index_groups=groups)
    (out,) = call(z_sum_kernel, [shape(rows, 128, **half)], out)
    groups = [[z * 8 + g for g in range(8)] for z in range(extent // 8)]
    out = lax.all_gather(out, "space", axis_index_groups=groups)
    sum_in, sum_atom, sum_basis, sum_out = call(
        functools.partial(final_kernel, grad_scale),
        [shape(512, 128), shape(256, 128), shape(64, 128), shape(512, 128)],
        out,
        scratch=[pltpu.VMEM((ROWS, 128), F32)],
    )
    return grad_edge, grad_atom, sum_in, sum_atom, sum_basis, sum_out


def solution(mesh):
    placed = (
        P("space", "col"),
        P("space", None),
        P("space", "col"),
        P("space", None),
        P(None, "col"),
        P(None, "col"),
        P(None, "col"),
        P(None, "col"),
        P("space"),
        P("space"),
        P("space"),
        P("space", None),
    )
    return jax.shard_map(
        body,
        mesh=mesh,
        in_specs=placed,
        out_specs=(
            P("space", "col"),
            P("space", None),
            P(None, "col"),
            P(None, "col"),
            P(None, "col"),
            P(None, "col"),
        ),
        check_vma=False,
    )
```

```python
import functools
import math

import jax
import jax.numpy as jnp
from jax import lax
from jax.experimental import pallas as pl
from jax.experimental.pallas import tpu as pltpu
from jax.sharding import PartitionSpec as P

F32 = jnp.float32
BF16 = jnp.bfloat16
VMEM = pl.BlockSpec(memory_space=pltpu.VMEM)
ROWS = 1408
STEP = 512


def call(kernel, outs, *args, scratch=(), flops=0):
    total = sum(math.prod(o.shape) * o.dtype.itemsize for o in outs)
    total += sum(a.size * a.dtype.itemsize for a in args)
    return pl.pallas_call(
        kernel,
        out_shape=list(outs),
        in_specs=[VMEM] * len(args),
        out_specs=[VMEM] * len(outs),
        scratch_shapes=list(scratch),
        compiler_params=pltpu.CompilerParams(vmem_limit_bytes=40 * 1024 * 1024),
        cost_estimate=pl.CostEstimate(flops=flops, bytes_accessed=total, transcendentals=0),
    )(*args)


def shape(*dims, dtype=F32):
    return jax.ShapeDtypeStruct(dims, dtype)


def dot(a, b, dims=((1,), (0,))):
    return lax.dot_general(a, b, (dims, ((), ())), preferred_element_type=F32)


def dot_nt(a, b):
    return dot(a, b, ((1,), (1,)))


def dot_tn(a, b):
    return dot(a, b, ((0,), (0,)))


def one_hot(mask):
    return jnp.where(mask, 1.0, 0.0).astype(BF16)


def iota(rows, lanes, axis):
    return lax.broadcasted_iota(jnp.int32, (rows, lanes), axis)


def block_of(ref, index):
    return ref[pl.ds(pl.multiple_of(index * 128, 128), 128), :]


def near(distance):
    return lax.axis_index("col") ^ distance


def bit_of(level):
    return lax.rem(lax.axis_index("space") // (1 << level), 2)


def sigmoid(value):
    return 1.0 / (1.0 + jnp.exp(-value))


def edge_kernel(
    edge_ref, atom_ref, win_ref, watom_ref, index_ref, send_ref,
    pre_ref, act_ref, out_ref, ae_ref,
):
    index = index_ref[...]
    at = one_hot(iota(8, 128, 0) == index)
    atom_edge = dot_tn(at, atom_ref[...]).astype(BF16)
    ae_ref[...] = atom_edge
    pre = dot(atom_edge, watom_ref[...])
    for c in range(4):
        pre = pre + dot(edge_ref[c], win_ref[c * 128 : (c + 1) * 128, :])
    pre_ref[...] = pre
    act = (pre * sigmoid(pre)).astype(BF16)
    act_ref[...] = act
    for i in range(8):
        pick = one_hot(iota(128, 128, 0) == send_ref[i : i + 1, :])
        out_ref[i * 128 : (i + 1) * 128, :] = dot_tn(pick, act).astype(BF16)


def pack_kernel(cot_ref, wout_ref, after_ref, out_ref):
    out_ref[:128, :] = cot_ref[...]
    out_ref[128:, :] = wout_ref[...]


def scatter_kernel(
    gather_ref, basis_ref, wb_ref, source_ref, target_ref,
    gm_ref, own_ref, halo_ref, acc_ref,
):
    mine = pl.ds(pl.multiple_of(lax.axis_index("col") * 128 + 128, 128), 128)
    total = dot_nt(gather_ref[0, :128, :], gather_ref[0, mine, :])
    for c in range(1, 4):
        total = total + dot_nt(gather_ref[c, :128, :], gather_ref[c, mine, :])
    gm = total.astype(BF16)
    gm_ref[...] = gm
    wb = wb_ref[...]
    rows = acc_ref.shape[0]
    for c in range(source_ref.shape[0] * 128 // STEP):
        lines = range(c * STEP // 128, (c + 1) * STEP // 128)
        basis = basis_ref[:, c * STEP : (c + 1) * STEP]
        bv = dot_tn(basis, wb)
        sel = jnp.concatenate(
            [one_hot(iota(128, 128, 0) == target_ref[i : i + 1, :]) for i in lines], axis=1
        )
        spread = dot_tn(sel, gm)
        exact = spread * bv
        high = exact.astype(BF16)
        low = (exact - high.astype(F32)).astype(BF16)
        put = jnp.concatenate(
            [one_hot(iota(rows, 128, 0) == source_ref[i : i + 1, :]) for i in lines], axis=1
        )
        both = dot(put, jnp.concatenate([high, low], axis=1))
        part = both[:, :128] + both[:, 128:]
        if c == 0:
            acc_ref[...] = part
        else:
            acc_ref[...] += part
    own_ref[...] = acc_ref[:128, :]
    halo_ref[...] = acc_ref[128:, :].astype(BF16)


def gather_kernel(
    act_ref, in_ref, gm_ref, basis_ref, wb_ref, source_ref, target_ref,
    msg_ref, bw_ref, ext_ref,
):
    ext_ref[:128, :] = act_ref[...]
    ext_ref[128:, :] = in_ref[...]
    ext = ext_ref[...]
    gm = gm_ref[...]
    wb = wb_ref[...]
    rows = ext_ref.shape[0]
    msg = jnp.zeros((128, 128), F32)
    bw = jnp.zeros(bw_ref.shape, F32)
    for c in range(source_ref.shape[0] * 128 // STEP):
        lines = range(c * STEP // 128, (c + 1) * STEP // 128)
        basis = basis_ref[:, c * STEP : (c + 1) * STEP]
        bv = dot_tn(basis, wb)
        sel = jnp.concatenate(
            [one_hot(iota(128, 128, 0) == target_ref[i : i + 1, :]) for i in lines], axis=1
        )
        spread = dot_tn(sel, gm)
        cols = jnp.concatenate(
            [jnp.broadcast_to(source_ref[i : i + 1, :], (128, 128)).T for i in lines], axis=0
        )
        pick = jnp.concatenate(
            [one_hot(cols == iota(STEP, 128, 1) + 128 * k) for k in range(rows // 128)], axis=1
        )
        z = dot(pick, ext)
        msg = msg + dot(sel, (bv * z).astype(BF16))
        bw = bw + dot(basis, (spread * z).astype(BF16))
    msg_ref[...] = msg.astype(BF16)
    bw_ref[...] = bw


def weight_kernel(
    ret_ref, own_ref, pre_ref, send_ref, edge_ref, ae_ref, win_ref, watom_ref, index_ref,
    msg_ref, cot_ref, bw_ref,
    out_ref, keep_ref, edge_own, atom_own, col1, col2, col3, acc_ref,
):
    ga = own_ref[...]
    for i in range(8):
        put = one_hot(iota(128, 128, 0) == send_ref[i : i + 1, :])
        ga = ga + dot(put, ret_ref[i * 128 : (i + 1) * 128, :])
    pre = pre_ref[...]
    sig = sigmoid(pre)
    gp = (ga * (sig * (1.0 + pre * (1.0 - sig)))).astype(BF16)
    cot = cot_ref[...]
    for c in range(4):
        acc_ref[c * 128 : (c + 1) * 128, :] = dot_tn(edge_ref[c], gp)
        acc_ref[768 + c * 128 : 896 + c * 128, :] = dot_tn(msg_ref[c], cot)
    acc_ref[512:768, :] = dot_tn(ae_ref[...], gp)
    acc_ref[1280:1344, :] = bw_ref[...]
    acc_ref[1344:, :] = jnp.zeros((ROWS - 1344, 128), F32)
    half = ROWS // 2
    mine = pl.multiple_of(bit_of(0) * half, 16)
    other = pl.multiple_of(half - mine, 16)
    keep_ref[...] = acc_ref[pl.ds(mine, half), :]
    out_ref[...] = acc_ref[pl.ds(other, half), :].astype(BF16)
    at = one_hot(iota(8, 128, 0) == index_ref[...])
    total = dot(at, gp)
    high = total.astype(BF16)
    low = (total - high.astype(F32)).astype(BF16)
    atom = dot_nt(high, watom_ref[...]) + dot_nt(low, watom_ref[...])
    edge_own[...] = dot_nt(gp, block_of(win_ref, near(0)))
    atom = jnp.concatenate([atom[:, :128], atom[:, 128:]], axis=0)
    high = atom.astype(BF16)
    low = (atom - high.astype(F32)).astype(BF16)
    atom_own[...] = high.astype(F32) + low.astype(F32)
    for d, ref in ((1, col1), (2, col2), (3, col3)):
        ref[:128, :] = dot_nt(gp, block_of(win_ref, near(d))).astype(BF16)
        ref[128:144, :] = high
        ref[144:, :] = low


def col_final_kernel(edge_own, atom_own, got1, got2, got3, edge_ref, atom_ref):
    edge = edge_own[...]
    atom = atom_own[...]
    for got in (got1, got2, got3):
        edge = edge + got[:128, :].astype(F32)
        atom = atom + (got[128:144, :].astype(F32) + got[144:, :].astype(F32))
    edge_ref[...] = edge.astype(BF16)
    atom_ref[:, :128] = atom[:8, :]
    atom_ref[:, 128:] = atom[8:, :]


def halve_kernel(level, keep_ref, got_ref, after_ref, send_ref, own_ref):
    half = send_ref.shape[0]
    mine = pl.multiple_of(bit_of(level) * half, 16)
    other = pl.multiple_of(half - mine, 16)
    send_ref[...] = (
        keep_ref[pl.ds(other, half), :] + got_ref[pl.ds(other, half), :].astype(F32)
    ).astype(BF16)
    own_ref[...] = keep_ref[pl.ds(mine, half), :] + got_ref[pl.ds(mine, half), :].astype(F32)


def add_kernel(own_ref, got_ref, after2, after3, out_ref):
    out_ref[...] = (own_ref[...] + got_ref[...].astype(F32)).astype(BF16)


def z_sum_kernel(all_ref, out_ref):
    total = all_ref[0].astype(F32)
    for i in range(1, all_ref.shape[0]):
        total = total + all_ref[i].astype(F32)
    out_ref[...] = total.astype(BF16)


def final_kernel(scale, all_ref, win_ref, watom_ref, wb_ref, wout_ref, acc_ref):
    rows = all_ref.shape[1]
    for g in range(8):
        place = ((g % 2) * 4 + (g // 2 % 2) * 2 + g // 4) * rows
        acc_ref[place : place + rows, :] = all_ref[g].astype(F32) * scale
    win_ref[...] = acc_ref[:512, :]
    watom_ref[...] = acc_ref[512:768, :]
    wout_ref[...] = acc_ref[768:1280, :]
    wb_ref[...] = acc_ref[1280:1344, :]


def col_swap(array, distance):
    return lax.ppermute(array, "col", [(i, i ^ distance) for i in range(4)])


def space_swap(array, distance, extent):
    return lax.ppermute(array, "space", [(i, i ^ distance) for i in range(extent)])


def body(
    edge_embed,
    atom_embed,
    cotangent,
    trip_basis,
    weight_in,
    weight_atom,
    weight_basis,
    weight_out,
    atom_index,
    trip_source,
    trip_target,
    send_rows,
):
    extent = lax.axis_size("space")
    grad_scale = 1.0 / math.sqrt(edge_embed.shape[0] * extent)
    half = dict(dtype=BF16)
    source = trip_source.reshape(-1, 128)
    target = trip_target.reshape(-1, 128)
    send = send_rows.reshape(8, 128)
    index = atom_index.reshape(1, 128)

    basis = trip_basis.T
    edge_all = lax.all_gather(edge_embed, "col")
    preact, active, outgoing, atom_edge = call(
        edge_kernel,
        [shape(128, 128), shape(128, 128, **half), shape(1024, 128, **half), shape(128, 256, **half)],
        edge_all, atom_embed, weight_in, weight_atom, index, send,
    )
    incoming = lax.all_to_all(
        outgoing.reshape(extent, 8, 128), "space", split_axis=0, concat_axis=0, tiled=True
    ).reshape(1024, 128)
    (cot_wout,) = call(pack_kernel, [shape(640, 128, **half)], cotangent, weight_out, active)
    cot_wout = lax.all_gather(cot_wout, "col")
    grad_msg, grad_own, grad_halo = call(
        scatter_kernel,
        [shape(128, 128, **half), shape(128, 128), shape(1024, 128, **half)],
        cot_wout, basis, weight_basis, source, target,
        scratch=[pltpu.VMEM((1152, 128), F32)],
        flops=2 * 4096 * 1152 * 128,
    )
    returned = lax.all_to_all(
        grad_halo.reshape(extent, 8, 128), "space", split_axis=0, concat_axis=0, tiled=True
    ).reshape(1024, 128)
    message, grad_bw = call(
        gather_kernel,
        [shape(128, 128, **half), shape(64, 128)],
        active, incoming, grad_msg, basis, weight_basis, source, target,
        scratch=[pltpu.VMEM((1152, 128), BF16)],
        flops=2 * 4096 * 1152 * 128,
    )
    msg_all = lax.all_gather(message, "col")
    out, keep, edge_own, atom_own, col1, col2, col3 = call(
        weight_kernel,
        [
            shape(ROWS // 2, 128, **half), shape(ROWS // 2, 128), shape(128, 128), shape(16, 128),
            shape(160, 128, **half), shape(160, 128, **half), shape(160, 128, **half),
        ],
        returned, grad_own, preact, send, edge_all, atom_edge, weight_in, weight_atom, index,
        msg_all, cotangent, grad_bw,
        scratch=[pltpu.VMEM((ROWS, 128), F32)],
    )
    rows = ROWS // 2
    got1, got2, got3 = (col_swap(part, d) for d, part in ((1, col1), (2, col2), (3, col3)))
    for level, after in ((1, edge_own), (2, got1)):
        rows //= 2
        got = space_swap(out, 1 << (level - 1), extent)
        out, keep = call(
            functools.partial(halve_kernel, level),
            [shape(rows, 128, **half), shape(rows, 128)],
            keep, got, after,
        )
    (out,) = call(
        add_kernel, [shape(rows, 128, **half)], keep, space_swap(out, 4, extent), got2, got3
    )
    grad_edge, grad_atom = call(
        col_final_kernel, [shape(128, 128, **half), shape(8, 256)],
        edge_own, atom_own, got1, got2, got3,
    )
    depth = extent // 8
    groups = [
        [(z if g % 2 == 0 else depth - 1 - z) * 8 + g for z in range(depth)] for g in range(8)
    ]
    out = lax.all_gather(out, "space", axis_index_groups=groups)
    (out,) = call(z_sum_kernel, [shape(rows, 128, **half)], out)
    groups = [[z * 8 + g for g in range(8)] for z in range(depth)]
    out = lax.all_gather(out, "space", axis_index_groups=groups)
    sum_in, sum_atom, sum_basis, sum_out = call(
        functools.partial(final_kernel, grad_scale),
        [shape(512, 128), shape(256, 128), shape(64, 128), shape(512, 128)],
        out,
        scratch=[pltpu.VMEM((ROWS, 128), F32)],
    )
    return grad_edge, grad_atom, sum_in, sum_atom, sum_basis, sum_out


def solution(mesh):
    placed = (
        P("space", "col"),
        P("space", None),
        P("space", "col"),
        P("space", None),
        P(None, "col"),
        P(None, "col"),
        P(None, "col"),
        P(None, "col"),
        P("space"),
        P("space"),
        P("space"),
        P("space", None),
    )
    return jax.shard_map(
        body,
        mesh=mesh,
        in_specs=placed,
        out_specs=(
            P("space", "col"),
            P("space", None),
            P(None, "col"),
            P(None, "col"),
            P(None, "col"),
            P(None, "col"),
        ),
        check_vma=False,
    )
```

```python
import functools
import math

import jax
import jax.numpy as jnp
from jax import lax
from jax.experimental import pallas as pl
from jax.experimental.pallas import tpu as pltpu
from jax.sharding import PartitionSpec as P

F32 = jnp.float32
BF16 = jnp.bfloat16
VMEM = pl.BlockSpec(memory_space=pltpu.VMEM)
ROWS = 1408
STEP = 512


def call(kernel, outs, *args, scratch=(), flops=0, limit=20):
    total = sum(math.prod(o.shape) * o.dtype.itemsize for o in outs)
    total += sum(a.size * a.dtype.itemsize for a in args)
    return pl.pallas_call(
        kernel,
        out_shape=list(outs),
        in_specs=[VMEM] * len(args),
        out_specs=[VMEM] * len(outs),
        scratch_shapes=list(scratch),
        compiler_params=pltpu.CompilerParams(vmem_limit_bytes=limit * 1024 * 1024),
        cost_estimate=pl.CostEstimate(flops=flops, bytes_accessed=total, transcendentals=0),
    )(*args)


def shape(*dims, dtype=F32):
    return jax.ShapeDtypeStruct(dims, dtype)


def dot(a, b, dims=((1,), (0,))):
    return lax.dot_general(a, b, (dims, ((), ())), preferred_element_type=F32)


def dot_nt(a, b):
    return dot(a, b, ((1,), (1,)))


def dot_tn(a, b):
    return dot(a, b, ((0,), (0,)))


def one_hot(mask):
    return jnp.where(mask, 1.0, 0.0).astype(BF16)


def iota(rows, lanes, axis):
    return lax.broadcasted_iota(jnp.int32, (rows, lanes), axis)


def bit_of(level):
    return lax.rem(lax.axis_index("space") // (1 << level), 2)


def sigmoid(value):
    return 1.0 / (1.0 + jnp.exp(-value))


def pack_kernel(edge_ref, cot_ref, wout_ref, out_ref):
    out_ref[:128, :] = edge_ref[...]
    out_ref[128:256, :] = cot_ref[...]
    out_ref[256:, :] = wout_ref[...]


def pack_weights_kernel(win_ref, watom_ref, after_ref, out_ref):
    out_ref[:512, :] = win_ref[...]
    out_ref[512:, :] = watom_ref[...]


def target_mask(target_ref, lines):
    return jnp.concatenate(
        [one_hot(iota(128, 128, 0) == target_ref[i : i + 1, :]) for i in lines], axis=1
    )


def steps(source_ref):
    for c in range(source_ref.shape[0] * 128 // STEP):
        yield slice(c * STEP, (c + 1) * STEP), range(c * STEP // 128, (c + 1) * STEP // 128)


def front_kernel(
    all_ref, atom_ref, win_ref, watom_ref, index_ref, send_ref, basis_ref, wb_ref, source_ref,
    target_ref,
    pre_ref, act_ref, ae_ref, gm_ref, own_ref, both_ref, acc_ref,
):
    at = one_hot(iota(8, 128, 0) == index_ref[...])
    atom_edge = dot_tn(at, atom_ref[...]).astype(BF16)
    ae_ref[...] = atom_edge
    pre = dot(atom_edge, watom_ref[...])
    mine = pl.ds(pl.multiple_of(lax.axis_index("col") * 128 + 256, 128), 128)
    total = jnp.zeros((128, 128), F32)
    for c in range(4):
        pre = pre + dot(all_ref[c, :128, :], win_ref[c * 128 : (c + 1) * 128, :])
        total = total + dot_nt(all_ref[c, 128:256, :], all_ref[c, mine, :])
    pre_ref[...] = pre
    act = (pre * sigmoid(pre)).astype(BF16)
    act_ref[...] = act
    gm = total.astype(BF16)
    gm_ref[...] = gm
    wb = wb_ref[...]
    rows = acc_ref.shape[0]
    for span, lines in steps(source_ref):
        exact = dot_tn(target_mask(target_ref, lines), gm) * dot_tn(basis_ref[:, span], wb)
        high = exact.astype(BF16)
        low = (exact - high.astype(F32)).astype(BF16)
        put = jnp.concatenate(
            [one_hot(iota(rows, 128, 0) == source_ref[i : i + 1, :]) for i in lines], axis=1
        )
        two = dot(put, jnp.concatenate([high, low], axis=1))
        part = two[:, :128] + two[:, 128:]
        if span.start == 0:
            acc_ref[...] = part
        else:
            acc_ref[...] += part
    own_ref[...] = acc_ref[:128, :]
    for i in range(8):
        pick = one_hot(iota(128, 128, 0) == send_ref[i : i + 1, :])
        outgoing = dot_tn(pick, act).reshape(16, 8, 128)
        back = acc_ref[(i + 1) * 128 : (i + 2) * 128, :].reshape(16, 8, 128)
        both_ref[i * 256 : (i + 1) * 256, :] = (
            jnp.concatenate([outgoing, back], axis=1).reshape(256, 128).astype(BF16)
        )


def gather_kernel(
    act_ref, in_ref, own_ref, pre_ref, send_ref, gm_ref, basis_ref, wb_ref, source_ref, target_ref,
    after_ref,
    pair_ref, bw_ref, ext_ref,
):
    got = in_ref[...].astype(F32).reshape(-1, 16, 128)
    ext_ref[:128, :] = act_ref[...]
    ext_ref[128:, :] = got[:, :8, :].reshape(-1, 128).astype(BF16)
    back = got[:, 8:, :].reshape(-1, 128).astype(BF16)
    ga = own_ref[...]
    for i in range(8):
        put = one_hot(iota(128, 128, 0) == send_ref[i : i + 1, :])
        ga = ga + dot(put, back[i * 128 : (i + 1) * 128, :])
    pre = pre_ref[...]
    sig = sigmoid(pre)
    pair_ref[128:, :] = (ga * (sig * (1.0 + pre * (1.0 - sig)))).astype(BF16)
    ext = ext_ref[...]
    msg = jnp.zeros((128, 128), F32)
    bw = jnp.zeros(bw_ref.shape, F32)
    gm = gm_ref[...]
    wb = wb_ref[...]
    for span, lines in steps(source_ref):
        basis = basis_ref[:, span]
        mask = target_mask(target_ref, lines)
        cols = jnp.concatenate(
            [jnp.broadcast_to(source_ref[i : i + 1, :], (128, 128)).T for i in lines], axis=0
        )
        pick = jnp.concatenate(
            [
                one_hot(cols == iota(STEP, 128, 1) + 128 * k)
                for k in range(ext_ref.shape[0] // 128)
            ],
            axis=1,
        )
        z = dot(pick, ext)
        msg = msg + dot(mask, (dot_tn(basis, wb) * z).astype(BF16))
        bw = bw + dot(basis, (dot_tn(mask, gm) * z).astype(BF16))
    pair_ref[:128, :] = msg.astype(BF16)
    bw_ref[...] = bw


def weight_kernel(all_ref, pair_all, pair_ref, ae_ref, cot_ref, bw_ref, out_ref, keep_ref, acc_ref):
    gp = pair_ref[128:, :]
    cot = cot_ref[...]
    for c in range(4):
        acc_ref[c * 128 : (c + 1) * 128, :] = dot_tn(all_ref[c, :128, :], gp)
        acc_ref[768 + c * 128 : 896 + c * 128, :] = dot_tn(pair_all[c, :128, :], cot)
    acc_ref[512:768, :] = dot_tn(ae_ref[...], gp)
    acc_ref[1280:1344, :] = bw_ref[...]
    acc_ref[1344:, :] = jnp.zeros((ROWS - 1344, 128), F32)
    half = ROWS // 2
    mine = pl.multiple_of(bit_of(0) * half, 16)
    other = pl.multiple_of(half - mine, 16)
    keep_ref[...] = acc_ref[pl.ds(mine, half), :]
    out_ref[...] = acc_ref[pl.ds(other, half), :].astype(BF16)


def edge_out_kernel(pair_all, weights_ref, index_ref, edge_ref, atom_ref):
    mine = pl.ds(pl.multiple_of(lax.axis_index("col") * 128, 128), 128)
    at = one_hot(iota(8, 128, 0) == index_ref[...])
    edge = jnp.zeros((128, 128), F32)
    atom = jnp.zeros((8, 256), F32)
    for c in range(4):
        gp = pair_all[c, 128:, :]
        edge = edge + dot_nt(gp, weights_ref[c, mine, :])
        total = dot(at, gp)
        high = total.astype(BF16)
        low = (total - high.astype(F32)).astype(BF16)
        atom = atom + dot_nt(high, weights_ref[c, 512:, :]) + dot_nt(low, weights_ref[c, 512:, :])
    edge_ref[...] = edge.astype(BF16)
    atom_ref[...] = atom


def halve_kernel(level, keep_ref, got_ref, send_ref, own_ref):
    half = send_ref.shape[0]
    mine = pl.multiple_of(bit_of(level) * half, 16)
    other = pl.multiple_of(half - mine, 16)
    send_ref[...] = (
        keep_ref[pl.ds(other, half), :] + got_ref[pl.ds(other, half), :].astype(F32)
    ).astype(BF16)
    own_ref[...] = keep_ref[pl.ds(mine, half), :] + got_ref[pl.ds(mine, half), :].astype(F32)


def add_kernel(own_ref, got_ref, after_ref, out_ref):
    out_ref[...] = (own_ref[...] + got_ref[...].astype(F32)).astype(BF16)


def z_sum_kernel(all_ref, out_ref):
    total = all_ref[0].astype(F32)
    for i in range(1, all_ref.shape[0]):
        total = total + all_ref[i].astype(F32)
    out_ref[...] = total.astype(BF16)


def final_kernel(scale, all_ref, win_ref, watom_ref, wb_ref, wout_ref, acc_ref):
    rows = all_ref.shape[1]
    for g in range(8):
        place = ((g % 2) * 4 + (g // 2 % 2) * 2 + g // 4) * rows
        acc_ref[place : place + rows, :] = all_ref[g].astype(F32) * scale
    win_ref[...] = acc_ref[:512, :]
    watom_ref[...] = acc_ref[512:768, :]
    wout_ref[...] = acc_ref[768:1280, :]
    wb_ref[...] = acc_ref[1280:1344, :]


def space_swap(array, distance, extent):
    return lax.ppermute(array, "space", [(i, i ^ distance) for i in range(extent)])


def body(
    edge_embed,
    atom_embed,
    cotangent,
    trip_basis,
    weight_in,
    weight_atom,
    weight_basis,
    weight_out,
    atom_index,
    trip_source,
    trip_target,
    send_rows,
):
    extent = lax.axis_size("space")
    grad_scale = 1.0 / math.sqrt(edge_embed.shape[0] * extent)
    half = dict(dtype=BF16)
    source = trip_source.reshape(-1, 128)
    target = trip_target.reshape(-1, 128)
    send = send_rows.reshape(8, 128)
    index = atom_index.reshape(1, 128)

    basis = trip_basis.T
    (packed,) = call(
        pack_kernel, [shape(768, 128, **half)], edge_embed, cotangent, weight_out, limit=58
    )
    col_all = lax.all_gather(packed, "col")
    preact, active, atom_edge, grad_msg, grad_own, both = call(
        front_kernel,
        [
            shape(128, 128), shape(128, 128, **half), shape(128, 256, **half),
            shape(128, 128, **half), shape(128, 128), shape(2048, 128, **half),
        ],
        col_all, atom_embed, weight_in, weight_atom, index, send, basis, weight_basis, source, target,
        scratch=[pltpu.VMEM((1152, 128), F32)],
        flops=2 * 4096 * 1152 * 128,
        limit=58,
    )
    both = lax.all_to_all(
        both.reshape(extent, 16, 128), "space", split_axis=0, concat_axis=0, tiled=True
    ).reshape(2048, 128)
    (weights,) = call(
        pack_weights_kernel, [shape(768, 128, **half)], weight_in, weight_atom, grad_own
    )
    weights = lax.all_gather(weights, "col")
    pair, grad_bw = call(
        gather_kernel,
        [shape(256, 128, **half), shape(64, 128)],
        active, both, grad_own, preact, send, grad_msg, basis, weight_basis, source, target, weights,
        scratch=[pltpu.VMEM((1152, 128), BF16)],
        flops=2 * 4096 * 1152 * 128,
        limit=58,
    )
    pair_all = lax.all_gather(pair, "col")
    out, keep = call(
        weight_kernel,
        [shape(ROWS // 2, 128, **half), shape(ROWS // 2, 128)],
        col_all, pair_all, pair, atom_edge, cotangent, grad_bw,
        scratch=[pltpu.VMEM((ROWS, 128), F32)],
    )
    grad_edge, grad_atom = call(
        edge_out_kernel, [shape(128, 128, **half), shape(8, 256)], pair_all, weights, index
    )
    rows = ROWS // 2
    for level in (1, 2):
        rows //= 2
        got = space_swap(out, 1 << (level - 1), extent)
        out, keep = call(
            functools.partial(halve_kernel, level),
            [shape(rows, 128, **half), shape(rows, 128)],
            keep, got,
        )
    (out,) = call(
        add_kernel, [shape(rows, 128, **half)], keep, space_swap(out, 4, extent), grad_atom
    )
    depth = extent // 8
    groups = [[z * 8 + g for z in range(depth)] for g in range(8)]
    out = lax.all_gather(out, "space", axis_index_groups=groups)
    (out,) = call(z_sum_kernel, [shape(rows, 128, **half)], out)
    groups = [[z * 8 + g for g in range(8)] for z in range(depth)]
    out = lax.all_gather(out, "space", axis_index_groups=groups)
    sum_in, sum_atom, sum_basis, sum_out = call(
        functools.partial(final_kernel, grad_scale),
        [shape(512, 128), shape(256, 128), shape(64, 128), shape(512, 128)],
        out,
        scratch=[pltpu.VMEM((ROWS, 128), F32)],
    )
    return grad_edge, grad_atom, sum_in, sum_atom, sum_basis, sum_out


def solution(mesh):
    placed = (
        P("space", "col"),
        P("space", None),
        P("space", "col"),
        P("space", None),
        P(None, "col"),
        P(None, "col"),
        P(None, "col"),
        P(None, "col"),
        P("space"),
        P("space"),
        P("space"),
        P("space", None),
    )
    return jax.shard_map(
        body,
        mesh=mesh,
        in_specs=placed,
        out_specs=(
            P("space", "col"),
            P("space", None),
            P(None, "col"),
            P(None, "col"),
            P(None, "col"),
            P(None, "col"),
        ),
        check_vma=False,
    )
```

```python
import functools
import math

import jax
import jax.numpy as jnp
from jax import lax
from jax.experimental import pallas as pl
from jax.experimental.pallas import tpu as pltpu
from jax.sharding import PartitionSpec as P

F32 = jnp.float32
BF16 = jnp.bfloat16
VMEM = pl.BlockSpec(memory_space=pltpu.VMEM)
ROWS = 1408
STEP = 2048


def call(kernel, outs, *args, scratch=(), flops=0, limit=20, after=()):
    total = sum(math.prod(o.shape) * o.dtype.itemsize for o in outs)
    total += sum(a.size * a.dtype.itemsize for a in args)
    return pl.pallas_call(
        kernel,
        out_shape=list(outs),
        in_specs=[VMEM] * len(args) + [pl.BlockSpec(memory_space=pl.ANY)] * len(after),
        out_specs=[VMEM] * len(outs),
        scratch_shapes=list(scratch),
        compiler_params=pltpu.CompilerParams(vmem_limit_bytes=limit * 1024 * 1024),
        cost_estimate=pl.CostEstimate(flops=flops, bytes_accessed=total, transcendentals=0),
    )(*args, *after)


def shape(*dims, dtype=F32):
    return jax.ShapeDtypeStruct(dims, dtype)


def dot(a, b, dims=((1,), (0,))):
    return lax.dot_general(a, b, (dims, ((), ())), preferred_element_type=F32)


def dot_nt(a, b):
    return dot(a, b, ((1,), (1,)))


def dot_tn(a, b):
    return dot(a, b, ((0,), (0,)))


def one_hot(mask):
    return jnp.where(mask, 1.0, 0.0).astype(BF16)


def iota(rows, lanes, axis):
    return lax.broadcasted_iota(jnp.int32, (rows, lanes), axis)


def bit_of(level):
    return lax.rem(lax.axis_index("space") // (1 << level), 2)


def sigmoid(value):
    return 1.0 / (1.0 + jnp.exp(-value))


def pack_kernel(edge_ref, cot_ref, wout_ref, out_ref):
    out_ref[:128, :] = edge_ref[...]
    out_ref[128:256, :] = cot_ref[...]
    out_ref[256:, :] = wout_ref[...]


def pack_weights_kernel(win_ref, watom_ref, after_ref, out_ref):
    out_ref[:512, :] = win_ref[...]
    out_ref[512:, :] = watom_ref[...]


def target_mask(target_ref, lines):
    return jnp.concatenate(
        [one_hot(iota(128, 128, 0) == target_ref[i : i + 1, :]) for i in lines], axis=1
    )


def steps(source_ref):
    for c in range(source_ref.shape[0] * 128 // STEP):
        yield slice(c * STEP, (c + 1) * STEP), range(c * STEP // 128, (c + 1) * STEP // 128)


def front_kernel(
    all_ref, atom_ref, win_ref, watom_ref, index_ref, send_ref, basis_ref, wb_ref, source_ref,
    target_ref,
    wide_ref, half_ref, ae_ref, both_ref, acc_ref,
):
    at = one_hot(iota(8, 128, 0) == index_ref[...])
    atom_edge = dot_tn(at, atom_ref[...]).astype(BF16)
    ae_ref[...] = atom_edge
    pre = dot(atom_edge, watom_ref[...])
    mine = pl.ds(pl.multiple_of(lax.axis_index("col") * 128 + 256, 128), 128)
    total = jnp.zeros((128, 128), F32)
    for c in range(4):
        pre = pre + dot(all_ref[c, :128, :], win_ref[c * 128 : (c + 1) * 128, :])
        total = total + dot_nt(all_ref[c, 128:256, :], all_ref[c, mine, :])
    wide_ref[:128, :] = pre
    act = (pre * sigmoid(pre)).astype(BF16)
    half_ref[:128, :] = act
    gm = total.astype(BF16)
    half_ref[128:, :] = gm
    wb = wb_ref[...]
    rows = acc_ref.shape[0]
    for span, lines in steps(source_ref):
        exact = dot_tn(target_mask(target_ref, lines), gm) * dot_tn(basis_ref[:, span], wb)
        high = exact.astype(BF16)
        low = (exact - high.astype(F32)).astype(BF16)
        put = jnp.concatenate(
            [one_hot(iota(rows, 128, 0) == source_ref[i : i + 1, :]) for i in lines], axis=1
        )
        two = dot(put, jnp.concatenate([high, low], axis=1))
        part = two[:, :128] + two[:, 128:]
        if span.start == 0:
            acc_ref[...] = part
        else:
            acc_ref[...] += part
    wide_ref[128:, :] = acc_ref[:128, :]
    for i in range(8):
        pick = one_hot(iota(128, 128, 0) == send_ref[i : i + 1, :])
        outgoing = dot_tn(pick, act).reshape(16, 8, 128)
        back = acc_ref[(i + 1) * 128 : (i + 2) * 128, :].reshape(16, 8, 128)
        both_ref[i * 256 : (i + 1) * 256, :] = (
            jnp.concatenate([outgoing, back], axis=1).reshape(256, 128).astype(BF16)
        )


def gather_kernel(
    half_ref, in_ref, wide_ref, send_ref, basis_ref, wb_ref, source_ref, target_ref,
    after_ref,
    pair_ref, bw_ref, ext_ref,
):
    got = in_ref[...].astype(F32).reshape(-1, 16, 128)
    ext_ref[:128, :] = half_ref[:128, :]
    ext_ref[128:, :] = got[:, :8, :].reshape(-1, 128).astype(BF16)
    back = got[:, 8:, :].reshape(-1, 128).astype(BF16)
    ga = wide_ref[128:, :]
    for i in range(8):
        put = one_hot(iota(128, 128, 0) == send_ref[i : i + 1, :])
        ga = ga + dot(put, back[i * 128 : (i + 1) * 128, :])
    pre = wide_ref[:128, :]
    sig = sigmoid(pre)
    pair_ref[128:, :] = (ga * (sig * (1.0 + pre * (1.0 - sig)))).astype(BF16)
    ext = ext_ref[...]
    msg = jnp.zeros((128, 128), F32)
    bw = jnp.zeros(bw_ref.shape, F32)
    gm = half_ref[128:, :]
    wb = wb_ref[...]
    for span, lines in steps(source_ref):
        basis = basis_ref[:, span]
        mask = target_mask(target_ref, lines)
        cols = jnp.concatenate(
            [jnp.broadcast_to(source_ref[i : i + 1, :], (128, 128)).T for i in lines], axis=0
        )
        pick = jnp.concatenate(
            [
                one_hot(cols == iota(STEP, 128, 1) + 128 * k)
                for k in range(ext_ref.shape[0] // 128)
            ],
            axis=1,
        )
        z = dot(pick, ext)
        msg = msg + dot(mask, (dot_tn(basis, wb) * z).astype(BF16))
        bw = bw + dot(basis, (dot_tn(mask, gm) * z).astype(BF16))
    pair_ref[:128, :] = msg.astype(BF16)
    bw_ref[...] = bw


def weight_kernel(all_ref, pair_all, pair_ref, ae_ref, cot_ref, bw_ref, out_ref, keep_ref, acc_ref):
    gp = pair_ref[128:, :]
    cot = cot_ref[...]
    for c in range(4):
        acc_ref[c * 128 : (c + 1) * 128, :] = dot_tn(all_ref[c, :128, :], gp)
        acc_ref[768 + c * 128 : 896 + c * 128, :] = dot_tn(pair_all[c, :128, :], cot)
    acc_ref[512:768, :] = dot_tn(ae_ref[...], gp)
    acc_ref[1280:1344, :] = bw_ref[...]
    acc_ref[1344:, :] = jnp.zeros((ROWS - 1344, 128), F32)
    half = ROWS // 2
    mine = pl.multiple_of(bit_of(0) * half, 16)
    other = pl.multiple_of(half - mine, 16)
    keep_ref[...] = acc_ref[pl.ds(mine, half), :]
    out_ref[...] = acc_ref[pl.ds(other, half), :].astype(BF16)


def edge_out_kernel(pair_all, weights_ref, index_ref, edge_ref, atom_ref, done_ref):
    mine = pl.ds(pl.multiple_of(lax.axis_index("col") * 128, 128), 128)
    at = one_hot(iota(8, 128, 0) == index_ref[...])
    edge = jnp.zeros((128, 128), F32)
    atom = jnp.zeros((8, 256), F32)
    for c in range(4):
        gp = pair_all[c, 128:, :]
        edge = edge + dot_nt(gp, weights_ref[c, mine, :])
        total = dot(at, gp)
        high = total.astype(BF16)
        low = (total - high.astype(F32)).astype(BF16)
        atom = atom + dot_nt(high, weights_ref[c, 512:, :]) + dot_nt(low, weights_ref[c, 512:, :])
    edge_ref[...] = edge.astype(BF16)
    atom_ref[...] = atom
    done_ref[...] = atom[:, :128]


def halve_kernel(level, keep_ref, got_ref, send_ref, own_ref):
    half = send_ref.shape[0]
    mine = pl.multiple_of(bit_of(level) * half, 16)
    other = pl.multiple_of(half - mine, 16)
    send_ref[...] = (
        keep_ref[pl.ds(other, half), :] + got_ref[pl.ds(other, half), :].astype(F32)
    ).astype(BF16)
    own_ref[...] = keep_ref[pl.ds(mine, half), :] + got_ref[pl.ds(mine, half), :].astype(F32)


def add_kernel(own_ref, got_ref, after_ref, out_ref):
    out_ref[...] = (own_ref[...] + got_ref[...].astype(F32)).astype(BF16)


def z_sum_kernel(all_ref, out_ref):
    total = all_ref[0].astype(F32)
    for i in range(1, all_ref.shape[0]):
        total = total + all_ref[i].astype(F32)
    out_ref[...] = total.astype(BF16)


def final_kernel(scale, all_ref, win_ref, watom_ref, wb_ref, wout_ref, acc_ref):
    rows = all_ref.shape[1]
    for g in range(8):
        place = ((g % 2) * 4 + (g // 2 % 2) * 2 + g // 4) * rows
        acc_ref[place : place + rows, :] = all_ref[g].astype(F32) * scale
    win_ref[...] = acc_ref[:512, :]
    watom_ref[...] = acc_ref[512:768, :]
    wout_ref[...] = acc_ref[768:1280, :]
    wb_ref[...] = acc_ref[1280:1344, :]


def space_swap(array, distance, extent):
    return lax.ppermute(array, "space", [(i, i ^ distance) for i in range(extent)])


def body(
    edge_embed,
    atom_embed,
    cotangent,
    trip_basis,
    weight_in,
    weight_atom,
    weight_basis,
    weight_out,
    atom_index,
    trip_source,
    trip_target,
    send_rows,
):
    extent = lax.axis_size("space")
    grad_scale = 1.0 / math.sqrt(edge_embed.shape[0] * extent)
    half = dict(dtype=BF16)
    source = trip_source.reshape(-1, 128)
    target = trip_target.reshape(-1, 128)
    send = send_rows.reshape(8, 128)
    index = atom_index.reshape(1, 128)

    basis = trip_basis.T
    (packed,) = call(
        pack_kernel, [shape(768, 128, **half)], edge_embed, cotangent, weight_out, limit=58
    )
    col_all = lax.all_gather(packed, "col")
    wide, narrow, atom_edge, both = call(
        front_kernel,
        [
            shape(256, 128), shape(256, 128, **half), shape(128, 256, **half),
            shape(2048, 128, **half),
        ],
        col_all, atom_embed, weight_in, weight_atom, index, send, basis, weight_basis, source, target,
        scratch=[pltpu.VMEM((1152, 128), F32)],
        flops=2 * 4096 * 1152 * 128,
        limit=58,
    )
    both = lax.all_to_all(
        both.reshape(extent, 16, 128), "space", split_axis=0, concat_axis=0, tiled=True
    ).reshape(2048, 128)
    (weights,) = call(
        pack_weights_kernel, [shape(768, 128, **half)], weight_in, weight_atom,
        after=(wide,),
    )
    weights = lax.all_gather(weights, "col")
    pair, grad_bw = call(
        gather_kernel,
        [shape(256, 128, **half), shape(64, 128)],
        narrow, both, wide, send, basis, weight_basis, source, target,
        scratch=[pltpu.VMEM((1152, 128), BF16)],
        flops=2 * 4096 * 1152 * 128,
        limit=50,
        after=(weights,),
    )
    pair_all = lax.all_gather(pair, "col")
    out, keep = call(
        weight_kernel,
        [shape(ROWS // 2, 128, **half), shape(ROWS // 2, 128)],
        col_all, pair_all, pair, atom_edge, cotangent, grad_bw,
        scratch=[pltpu.VMEM((ROWS, 128), F32)],
    )
    grad_edge, grad_atom, done = call(
        edge_out_kernel,
        [shape(128, 128, **half), shape(8, 256), shape(8, 128)],
        pair_all, weights, index,
    )
    rows = ROWS // 2
    for level in (1, 2):
        rows //= 2
        got = space_swap(out, 1 << (level - 1), extent)
        out, keep = call(
            functools.partial(halve_kernel, level),
            [shape(rows, 128, **half), shape(rows, 128)],
            keep, got,
        )
    (out,) = call(
        add_kernel, [shape(rows, 128, **half)], keep, space_swap(out, 4, extent),
        after=(done,),
    )
    depth = extent // 8
    groups = [[z * 8 + g for z in range(depth)] for g in range(8)]
    out = lax.all_gather(out, "space", axis_index_groups=groups)
    (out,) = call(z_sum_kernel, [shape(rows, 128, **half)], out)
    groups = [[z * 8 + g for g in range(8)] for z in range(depth)]
    out = lax.all_gather(out, "space", axis_index_groups=groups)
    sum_in, sum_atom, sum_basis, sum_out = call(
        functools.partial(final_kernel, grad_scale),
        [shape(512, 128), shape(256, 128), shape(64, 128), shape(512, 128)],
        out,
        scratch=[pltpu.VMEM((ROWS, 128), F32)],
    )
    return grad_edge, grad_atom, sum_in, sum_atom, sum_basis, sum_out


def solution(mesh):
    placed = (
        P("space", "col"),
        P("space", None),
        P("space", "col"),
        P("space", None),
        P(None, "col"),
        P(None, "col"),
        P(None, "col"),
        P(None, "col"),
        P("space"),
        P("space"),
        P("space"),
        P("space", None),
    )
    return jax.shard_map(
        body,
        mesh=mesh,
        in_specs=placed,
        out_specs=(
            P("space", "col"),
            P("space", None),
            P(None, "col"),
            P(None, "col"),
            P(None, "col"),
            P(None, "col"),
        ),
        check_vma=False,
    )
```

```python
import functools
import math

import jax
import jax.numpy as jnp
from jax import lax
from jax.experimental import pallas as pl
from jax.experimental.pallas import tpu as pltpu
from jax.sharding import PartitionSpec as P

F32 = jnp.float32
BF16 = jnp.bfloat16
VMEM = pl.BlockSpec(memory_space=pltpu.VMEM)
ROWS = 1408
STEP = 4096


def call(kernel, outs, *args, scratch=(), flops=0, limit=20, after=()):
    total = sum(math.prod(o.shape) * o.dtype.itemsize for o in outs)
    total += sum(a.size * a.dtype.itemsize for a in args)
    return pl.pallas_call(
        kernel,
        out_shape=list(outs),
        in_specs=[VMEM] * len(args) + [pl.BlockSpec(memory_space=pl.ANY)] * len(after),
        out_specs=[VMEM] * len(outs),
        scratch_shapes=list(scratch),
        compiler_params=pltpu.CompilerParams(vmem_limit_bytes=limit * 1024 * 1024),
        cost_estimate=pl.CostEstimate(flops=flops, bytes_accessed=total, transcendentals=0),
    )(*args, *after)


def shape(*dims, dtype=F32):
    return jax.ShapeDtypeStruct(dims, dtype)


def dot(a, b, dims=((1,), (0,))):
    return lax.dot_general(a, b, (dims, ((), ())), preferred_element_type=F32)


def dot_nt(a, b):
    return dot(a, b, ((1,), (1,)))


def dot_tn(a, b):
    return dot(a, b, ((0,), (0,)))


def one_hot(mask):
    return jnp.where(mask, 1.0, 0.0).astype(BF16)


def iota(rows, lanes, axis):
    return lax.broadcasted_iota(jnp.int32, (rows, lanes), axis)


def bit_of(level):
    return lax.rem(lax.axis_index("space") // (1 << level), 2)


def sigmoid(value):
    return 1.0 / (1.0 + jnp.exp(-value))


def pack_kernel(edge_ref, cot_ref, wout_ref, out_ref):
    out_ref[:128, :] = edge_ref[...]
    out_ref[128:256, :] = cot_ref[...]
    out_ref[256:, :] = wout_ref[...]


def pack_weights_kernel(win_ref, watom_ref, after_ref, out_ref):
    out_ref[:512, :] = win_ref[...]
    out_ref[512:, :] = watom_ref[...]


def target_mask(target_ref, lines):
    return jnp.concatenate(
        [one_hot(iota(128, 128, 0) == target_ref[i : i + 1, :]) for i in lines], axis=1
    )


def steps(source_ref):
    for c in range(source_ref.shape[0] * 128 // STEP):
        yield slice(c * STEP, (c + 1) * STEP), range(c * STEP // 128, (c + 1) * STEP // 128)


def front_kernel(
    all_ref, atom_ref, win_ref, watom_ref, index_ref, send_ref, basis_ref, wb_ref, source_ref,
    target_ref,
    wide_ref, half_ref, ae_ref, both_ref, acc_ref,
):
    at = one_hot(iota(8, 128, 0) == index_ref[...])
    atom_edge = dot_tn(at, atom_ref[...]).astype(BF16)
    ae_ref[...] = atom_edge
    pre = dot(atom_edge, watom_ref[...])
    mine = pl.ds(pl.multiple_of(lax.axis_index("col") * 128 + 256, 128), 128)
    total = jnp.zeros((128, 128), F32)
    for c in range(4):
        pre = pre + dot(all_ref[c, :128, :], win_ref[c * 128 : (c + 1) * 128, :])
        total = total + dot_nt(all_ref[c, 128:256, :], all_ref[c, mine, :])
    wide_ref[:128, :] = pre
    act = (pre * sigmoid(pre)).astype(BF16)
    half_ref[:128, :] = act
    gm = total.astype(BF16)
    half_ref[128:, :] = gm
    wb = wb_ref[...]
    rows = acc_ref.shape[0]
    for span, lines in steps(source_ref):
        exact = dot_tn(target_mask(target_ref, lines), gm) * dot_tn(basis_ref[:, span], wb)
        high = exact.astype(BF16)
        low = (exact - high.astype(F32)).astype(BF16)
        put = jnp.concatenate(
            [one_hot(iota(rows, 128, 0) == source_ref[i : i + 1, :]) for i in lines], axis=1
        )
        two = dot(put, jnp.concatenate([high, low], axis=1))
        part = two[:, :128] + two[:, 128:]
        if span.start == 0:
            acc_ref[...] = part
        else:
            acc_ref[...] += part
    wide_ref[128:, :] = acc_ref[:128, :]
    for i in range(8):
        pick = one_hot(iota(128, 128, 0) == send_ref[i : i + 1, :])
        outgoing = dot_tn(pick, act).reshape(16, 8, 128)
        back = acc_ref[(i + 1) * 128 : (i + 2) * 128, :].reshape(16, 8, 128)
        both_ref[i * 256 : (i + 1) * 256, :] = (
            jnp.concatenate([outgoing, back], axis=1).reshape(256, 128).astype(BF16)
        )


def gather_kernel(
    half_ref, in_ref, wide_ref, send_ref, basis_ref, wb_ref, source_ref, target_ref,
    after_ref,
    pair_ref, bw_ref, ext_ref,
):
    got = in_ref[...].astype(F32).reshape(-1, 16, 128)
    ext_ref[:128, :] = half_ref[:128, :]
    ext_ref[128:, :] = got[:, :8, :].reshape(-1, 128).astype(BF16)
    back = got[:, 8:, :].reshape(-1, 128).astype(BF16)
    ga = wide_ref[128:, :]
    for i in range(8):
        put = one_hot(iota(128, 128, 0) == send_ref[i : i + 1, :])
        ga = ga + dot(put, back[i * 128 : (i + 1) * 128, :])
    pre = wide_ref[:128, :]
    sig = sigmoid(pre)
    pair_ref[128:, :] = (ga * (sig * (1.0 + pre * (1.0 - sig)))).astype(BF16)
    ext = ext_ref[...]
    msg = jnp.zeros((128, 128), F32)
    bw = jnp.zeros(bw_ref.shape, F32)
    gm = half_ref[128:, :]
    wb = wb_ref[...]
    for span, lines in steps(source_ref):
        basis = basis_ref[:, span]
        mask = target_mask(target_ref, lines)
        cols = jnp.concatenate(
            [jnp.broadcast_to(source_ref[i : i + 1, :], (128, 128)).T for i in lines], axis=0
        )
        pick = jnp.concatenate(
            [
                one_hot(cols == iota(STEP, 128, 1) + 128 * k)
                for k in range(ext_ref.shape[0] // 128)
            ],
            axis=1,
        )
        z = dot(pick, ext)
        msg = msg + dot(mask, (dot_tn(basis, wb) * z).astype(BF16))
        bw = bw + dot(basis, (dot_tn(mask, gm) * z).astype(BF16))
    pair_ref[:128, :] = msg.astype(BF16)
    bw_ref[...] = bw


def weight_kernel(all_ref, pair_all, pair_ref, ae_ref, cot_ref, bw_ref, out_ref, keep_ref, acc_ref):
    gp = pair_ref[128:, :]
    cot = cot_ref[...]
    for c in range(4):
        acc_ref[c * 128 : (c + 1) * 128, :] = dot_tn(all_ref[c, :128, :], gp)
        acc_ref[768 + c * 128 : 896 + c * 128, :] = dot_tn(pair_all[c, :128, :], cot)
    acc_ref[512:768, :] = dot_tn(ae_ref[...], gp)
    acc_ref[1280:1344, :] = bw_ref[...]
    acc_ref[1344:, :] = jnp.zeros((ROWS - 1344, 128), F32)
    half = ROWS // 2
    mine = pl.multiple_of(bit_of(0) * half, 16)
    other = pl.multiple_of(half - mine, 16)
    keep_ref[...] = acc_ref[pl.ds(mine, half), :]
    out_ref[...] = acc_ref[pl.ds(other, half), :].astype(BF16)


def edge_out_kernel(pair_all, weights_ref, index_ref, edge_ref, atom_ref, done_ref):
    mine = pl.ds(pl.multiple_of(lax.axis_index("col") * 128, 128), 128)
    at = one_hot(iota(8, 128, 0) == index_ref[...])
    edge = jnp.zeros((128, 128), F32)
    atom = jnp.zeros((8, 256), F32)
    for c in range(4):
        gp = pair_all[c, 128:, :]
        edge = edge + dot_nt(gp, weights_ref[c, mine, :])
        total = dot(at, gp)
        high = total.astype(BF16)
        low = (total - high.astype(F32)).astype(BF16)
        atom = atom + dot_nt(high, weights_ref[c, 512:, :]) + dot_nt(low, weights_ref[c, 512:, :])
    edge_ref[...] = edge.astype(BF16)
    atom_ref[...] = atom
    done_ref[...] = atom[:, :128]


def halve_kernel(level, keep_ref, got_ref, *refs):
    send_ref, own_ref = refs[-2:]
    half = send_ref.shape[0]
    mine = pl.multiple_of(bit_of(level) * half, 16)
    other = pl.multiple_of(half - mine, 16)
    send_ref[...] = (
        keep_ref[pl.ds(other, half), :] + got_ref[pl.ds(other, half), :].astype(F32)
    ).astype(BF16)
    own_ref[...] = keep_ref[pl.ds(mine, half), :] + got_ref[pl.ds(mine, half), :].astype(F32)


def add_kernel(own_ref, got_ref, out_ref):
    out_ref[...] = (own_ref[...] + got_ref[...].astype(F32)).astype(BF16)


def z_sum_kernel(all_ref, out_ref):
    total = all_ref[0].astype(F32)
    for i in range(1, all_ref.shape[0]):
        total = total + all_ref[i].astype(F32)
    out_ref[...] = total.astype(BF16)


def final_kernel(scale, all_ref, win_ref, watom_ref, wb_ref, wout_ref, acc_ref):
    rows = all_ref.shape[1]
    for g in range(8):
        place = ((g % 2) * 4 + (g // 2 % 2) * 2 + g // 4) * rows
        acc_ref[place : place + rows, :] = all_ref[g].astype(F32) * scale
    win_ref[...] = acc_ref[:512, :]
    watom_ref[...] = acc_ref[512:768, :]
    wout_ref[...] = acc_ref[768:1280, :]
    wb_ref[...] = acc_ref[1280:1344, :]


def space_swap(array, distance, extent):
    return lax.ppermute(array, "space", [(i, i ^ distance) for i in range(extent)])


def body(
    edge_embed,
    atom_embed,
    cotangent,
    trip_basis,
    weight_in,
    weight_atom,
    weight_basis,
    weight_out,
    atom_index,
    trip_source,
    trip_target,
    send_rows,
):
    extent = lax.axis_size("space")
    grad_scale = 1.0 / math.sqrt(edge_embed.shape[0] * extent)
    half = dict(dtype=BF16)
    source = trip_source.reshape(-1, 128)
    target = trip_target.reshape(-1, 128)
    send = send_rows.reshape(8, 128)
    index = atom_index.reshape(1, 128)

    basis = trip_basis.T
    (packed,) = call(
        pack_kernel, [shape(768, 128, **half)], edge_embed, cotangent, weight_out, limit=58
    )
    col_all = lax.all_gather(packed, "col")
    wide, narrow, atom_edge, both = call(
        front_kernel,
        [
            shape(256, 128), shape(256, 128, **half), shape(128, 256, **half),
            shape(2048, 128, **half),
        ],
        col_all, atom_embed, weight_in, weight_atom, index, send, basis, weight_basis, source, target,
        scratch=[pltpu.VMEM((1152, 128), F32)],
        flops=2 * 4096 * 1152 * 128,
        limit=58,
    )
    both = lax.all_to_all(
        both.reshape(extent, 16, 128), "space", split_axis=0, concat_axis=0, tiled=True
    ).reshape(2048, 128)
    (weights,) = call(
        pack_weights_kernel, [shape(768, 128, **half)], weight_in, weight_atom,
        after=(wide,),
    )
    weights = lax.all_gather(weights, "col")
    pair, grad_bw = call(
        gather_kernel,
        [shape(256, 128, **half), shape(64, 128)],
        narrow, both, wide, send, basis, weight_basis, source, target,
        scratch=[pltpu.VMEM((1152, 128), BF16)],
        flops=2 * 4096 * 1152 * 128,
        limit=50,
        after=(weights,),
    )
    pair_all = lax.all_gather(pair, "col")
    out, keep = call(
        weight_kernel,
        [shape(ROWS // 2, 128, **half), shape(ROWS // 2, 128)],
        col_all, pair_all, pair, atom_edge, cotangent, grad_bw,
        scratch=[pltpu.VMEM((ROWS, 128), F32)],
    )
    grad_edge, grad_atom, done = call(
        edge_out_kernel,
        [shape(128, 128, **half), shape(8, 256), shape(8, 128)],
        pair_all, weights, index,
    )
    rows = ROWS // 2
    for level in (1, 2):
        rows //= 2
        got = space_swap(out, 1 << (level - 1), extent)
        out, keep = call(
            functools.partial(halve_kernel, level),
            [shape(rows, 128, **half), shape(rows, 128)],
            keep, got,
            after=(done,) if level == 2 else (),
        )
    (out,) = call(
        add_kernel, [shape(rows, 128, **half)], keep, space_swap(out, 4, extent)
    )
    depth = extent // 8
    groups = [[z * 8 + g for z in range(depth)] for g in range(8)]
    out = lax.all_gather(out, "space", axis_index_groups=groups)
    (out,) = call(z_sum_kernel, [shape(rows, 128, **half)], out)
    groups = [[z * 8 + g for g in range(8)] for z in range(depth)]
    out = lax.all_gather(out, "space", axis_index_groups=groups)
    sum_in, sum_atom, sum_basis, sum_out = call(
        functools.partial(final_kernel, grad_scale),
        [shape(512, 128), shape(256, 128), shape(64, 128), shape(512, 128)],
        out,
        scratch=[pltpu.VMEM((ROWS, 128), F32)],
    )
    return grad_edge, grad_atom, sum_in, sum_atom, sum_basis, sum_out


def solution(mesh):
    placed = (
        P("space", "col"),
        P("space", None),
        P("space", "col"),
        P("space", None),
        P(None, "col"),
        P(None, "col"),
        P(None, "col"),
        P(None, "col"),
        P("space"),
        P("space"),
        P("space"),
        P("space", None),
    )
    return jax.shard_map(
        body,
        mesh=mesh,
        in_specs=placed,
        out_specs=(
            P("space", "col"),
            P("space", None),
            P(None, "col"),
            P(None, "col"),
            P(None, "col"),
            P(None, "col"),
        ),
        check_vma=False,
    )
```
